32 devices in a mesh: parts: 2 (over y), region: 4 (over z), feat: 4 (over x, core).
Axes of the slice: x: 2, y: 2, z: 4, core: 2. Of those that a mesh axis runs over, the one named last changes fastest.
Arguments:
- grid_latent: bfloat16 [16384, 512], P(('parts', 'region')), parts along dimension 0, may hold values from -6 to 6
- mesh_latent: bfloat16 [4096, 512], P(('parts', 'region')), parts along dimension 0, may hold values from -6 to 6
- send_tiles: int32 [8, 4, 4], P(('parts', 'region')), parts along dimension 0, may hold values from -1 to 15, as said below
- g2m_sender: int32 [131072], P(('parts', 'region')), parts along dimension 0, may hold values from 0 to 2047, as said below
- g2m_receiver: int32 [131072], P(('parts', 'region')), parts along dimension 0, may hold values from -1 to 511, as said below
- g2m_feature: float32 [4, 131072], P(None, ('parts', 'region')), parts along dimension 1, may hold values from -6 to 6
- m2m_table: int32 [8, 4, 128], P(('parts', 'region')), parts along dimension 0, may hold values from -1 to 511, as said below
- m2m_sender: int32 [65536], P(('parts', 'region')), parts along dimension 0, may hold values from 0 to 511, as said below
- m2m_receiver: int32 [65536], P(('parts', 'region')), parts along dimension 0, may hold values from -1 to 511, as said below
- m2m_feature: float32 [4, 65536], P(None, ('parts', 'region')), parts along dimension 1, may hold values from -6 to 6
- w_send: bfloat16 [2, 512, 512], P(None, None, 'feat'), may hold values from -0.25 to 0.25
- w_recv: bfloat16 [2, 512, 512], P(None, None, 'feat'), may hold values from -0.25 to 0.25
- w_edge_feat: float32 [2, 4, 512], P(None, None, 'feat'), may hold values from -3 to 3
- b_edge: float32 [2, 512], P(None, 'feat'), may hold values from -6 to 6
- w_edge_out: bfloat16 [2, 512, 512], P(None, 'feat'), may hold values from -0.0625 to 0.0625
- b_edge_out: float32 [2, 512], replicated, may hold values from -3 to 3
- w_self: bfloat16 [2, 512, 512], P(None, None, 'feat'), may hold values from -0.25 to 0.25
- w_agg: bfloat16 [2, 512, 512], P(None, None, 'feat'), may hold values from -0.25 to 0.25
- b_node: float32 [2, 512], P(None, 'feat'), may hold values from -6 to 6
- w_node_out: bfloat16 [2, 512, 512], P(None, 'feat'), may hold values from -0.25 to 0.25
- b_node_out: float32 [2, 512], replicated, may hold values from -6 to 6
- norm_gain: float32 [2, 512], replicated, may hold values from 0.1 to 1.9
- norm_shift: float32 [2, 512], replicated, may hold values from -6 to 6
Outputs:
- mesh_encoded: bfloat16 [4096, 512], P(('parts', 'region'), 'feat'), parts along dimension 0
- mesh_processed: bfloat16 [4096, 512], P(('parts', 'region'), 'feat'), parts along dimension 0
The draws below stay inside these ranges and needn't reach their ends.
There are 2 independent parts, one for each index of `parts`. The reference program is written for one: setup_inputs(seed, part) draws one part's arguments, and reference() takes and returns one part's arrays. A program takes and returns all parts, laid end to end along the dimension named above; an argument that names none is the same for every part. Nothing has to cross between parts.
Inputs may be any that keep to these rules, and one draw needn't show every extreme that they name: `send_tiles`: entry [s, d, j] is a tile of region s (rows t * 128 to t * 128 + 127 of it) whose rows region d needs, or -1 for an empty slot; tiles of one [s, d] are distinct and used slots come first; every region uses all 4 slots for itself, and one region uses all 4 slots from every region. `g2m_sender`: an edge of region d names row r of slot j from region s with send_tiles[s, d, j] never -1. `g2m_receiver`: -1 marks an unused edge slot; one region has none. `m2m_table`: entry [d, s, j] is a local mesh node of region s whose sender term region d needs, or -1; distinct within one [d, s], used slots first; every region uses all 128 slots for itself, and one region uses all 128 slots from every region. `m2m_sender`: an edge of region d names slot j from region s with m2m_table[d, s, j] never -1. `m2m_receiver`: -1 marks an unused edge slot; one region has none.
All inputs are finite; a program needn't handle non-finite values.
Results may differ from the reference program's by a relative error of at most 0.018.
Values may be sent and summed in bfloat16 or wider, within the bound.
A program may use at most 64 MiB of HBM per device.

```python
import jax
import jax.numpy as jnp
from jax import lax

L = 512
H = 512
EF = 4
TILE = 128
TILES_DEV = 16
M_DEV = 512
G2M_DEV = 16384
M2M_DEV = 8192
CAP = 4
MCAP = 128
G_DEV = 2048
GRID = 8192
MESH = 2048
G2M = 65536
M2M = 32768
N_REGION = 4
N_FEAT = 4


def region_loads(key, capacity, salt):
    key = jax.random.fold_in(key, salt)
    first, second = jax.random.split(key)
    busiest = jax.random.randint(first, (), 0, N_REGION)
    counts = jax.random.randint(second, (N_REGION, N_REGION), 0, capacity + 1)
    source = jnp.arange(N_REGION)[:, None]
    target = jnp.arange(N_REGION)[None, :]
    full = (source == target) | (target == busiest)
    return (jnp.where(full, capacity, counts).astype(jnp.int32), busiest)


def distinct_picks(key, choices, capacity):
    scores = jax.random.randint(key, (N_REGION, N_REGION, choices), 0, 1 << 20) * choices + jnp.arange(choices)
    return jnp.argsort(scores, axis=-1)[:, :, :capacity].astype(jnp.int32)


def pick_live(key, live, per_region):
    slots = live.shape[1]
    order = jnp.argsort(jnp.where(live, 0, 1) * slots + jnp.arange(slots), axis=-1)
    used = jnp.sum(live.astype(jnp.int32), axis=-1)
    draws = jax.random.randint(key, (N_REGION, per_region), 0, 1 << 20) % used[:, None]
    return jnp.take_along_axis(order, draws, axis=-1).astype(jnp.int32)


def edge_targets(key, busiest, per_region, nodes):
    first, second = jax.random.split(key)
    targets = jax.random.randint(first, (N_REGION, per_region), 0, nodes)
    filled = jax.random.randint(second, (N_REGION,), per_region // 2, per_region + 1)
    filled = jnp.where(jnp.arange(N_REGION) == busiest, per_region, filled)
    result = jnp.where(jnp.arange(per_region)[None, :] < filled[:, None], targets, -1)
    return result.reshape(-1).astype(jnp.int32)


def set_last(values, busiest, top):
    row_hit = jnp.arange(values.shape[0])[:, None] == busiest
    col_hit = jnp.arange(values.shape[1])[None, :] == values.shape[1] - 1
    return jnp.where(row_hit & col_hit, top, values).astype(jnp.int32)


def draw_send_tiles(key, part):
    counts, busiest = region_loads(key, CAP, 101)
    key = jax.random.fold_in(key, 1)
    picks = distinct_picks(key, TILES_DEV, CAP)
    return jnp.where(jnp.arange(CAP)[None, None, :] < counts[:, :, None], picks, -1).astype(jnp.int32)


def draw_g2m_sender(key, part):
    counts, busiest = region_loads(key, CAP, 101)
    key = jax.random.fold_in(key, 2)
    first, second = jax.random.split(key)
    live = jnp.arange(CAP)[None, None, :] < jnp.transpose(counts)[:, :, None]
    chosen = pick_live(first, live.reshape(N_REGION, N_REGION * CAP), G2M_DEV)
    rows = jax.random.randint(second, (N_REGION, G2M_DEV), 0, TILE)
    values = set_last(chosen * TILE + rows, busiest, N_REGION * CAP * TILE - 1)
    return values.reshape(-1).astype(jnp.int32)


def draw_g2m_receiver(key, part):
    counts, busiest = region_loads(key, CAP, 101)
    key = jax.random.fold_in(key, 3)
    return edge_targets(key, busiest, G2M_DEV, M_DEV)


def draw_m2m_table(key, part):
    counts, busiest = region_loads(key, MCAP, 202)
    key = jax.random.fold_in(key, 4)
    picks = distinct_picks(key, M_DEV, MCAP)
    return jnp.where(jnp.arange(MCAP)[None, None, :] < jnp.transpose(counts)[:, :, None], picks, -1).astype(jnp.int32)


def draw_m2m_sender(key, part):
    counts, busiest = region_loads(key, MCAP, 202)
    key = jax.random.fold_in(key, 5)
    live = jnp.arange(MCAP)[None, None, :] < jnp.transpose(counts)[:, :, None]
    chosen = pick_live(key, live.reshape(N_REGION, N_REGION * MCAP), M2M_DEV)
    values = set_last(chosen, busiest, N_REGION * MCAP - 1)
    return values.reshape(-1).astype(jnp.int32)


def draw_m2m_receiver(key, part):
    counts, busiest = region_loads(key, MCAP, 202)
    key = jax.random.fold_in(key, 6)
    return edge_targets(key, busiest, M2M_DEV, M_DEV)


def level_of(own_key, shape, cuts, low, top_value):
    def one(position, shards_of):
        steps = jax.random.uniform(jax.random.fold_in(jax.random.fold_in(own_key, 6), position), (shards_of,), jnp.float32, low / len(cuts), top_value / len(cuts))
        return jnp.repeat(jnp.exp(steps), shape[position] // shards_of).reshape((-1,) + (1,) * (len(shape) - position - 1))

    loudness = one(*cuts[0])
    for cut in cuts[1:]:
        loudness = loudness * one(*cut)
    return loudness


def scatter_about(stream_key, extent, scale, most, shards=(), kind=jnp.bfloat16):
    drawn = scale * jax.random.normal(stream_key, extent, jnp.float32)
    if shards:
        drawn = drawn * level_of(stream_key, extent, shards, -0.22, 0.18)
    return jnp.clip(drawn, -most, most).astype(kind)


def setup_inputs(seed: int = 0, part: int = 0) -> dict:
    key_of = jax.random.split(jax.random.key(seed), 24)
    part_splits = jax.random.split(jax.random.fold_in(key_of[23], part), 24)
    return {
        "grid_latent": scatter_about(part_splits[0], (GRID, L), 1.0, 6.0, ((0, 4),)),
        "mesh_latent": scatter_about(part_splits[1], (MESH, L), 1.0, 6.0, ((0, 4),)),
        "send_tiles": draw_send_tiles(jax.random.fold_in(jax.random.fold_in(key_of[23], part), 71), part),
        "g2m_sender": draw_g2m_sender(jax.random.fold_in(jax.random.fold_in(key_of[23], part), 71), part),
        "g2m_receiver": draw_g2m_receiver(jax.random.fold_in(jax.random.fold_in(key_of[23], part), 71), part),
        "g2m_feature": scatter_about(part_splits[5], (EF, G2M), 1.0, 6.0, ((1, 4),), jnp.float32),
        "m2m_table": draw_m2m_table(jax.random.fold_in(jax.random.fold_in(key_of[23], part), 71), part),
        "m2m_sender": draw_m2m_sender(jax.random.fold_in(jax.random.fold_in(key_of[23], part), 71), part),
        "m2m_receiver": draw_m2m_receiver(jax.random.fold_in(jax.random.fold_in(key_of[23], part), 71), part),
        "m2m_feature": scatter_about(part_splits[9], (EF, M2M), 1.0, 6.0, ((1, 4),), jnp.float32),
        "w_send": scatter_about(key_of[10], (2, L, H), L ** -0.5, 0.25, ((2, 4),)),
        "w_recv": scatter_about(key_of[11], (2, L, H), L ** -0.5, 0.25, ((2, 4),)),
        "w_edge_feat": scatter_about(key_of[12], (2, EF, H), EF ** -0.5, 3.0, ((2, 4),), jnp.float32),
        "b_edge": scatter_about(key_of[13], (2, H), 1.0, 6.0, ((1, 4),), jnp.float32),
        "w_edge_out": scatter_about(key_of[14], (2, H, L), (16 * H) ** -0.5, 0.0625, ((1, 4),)),
        "b_edge_out": scatter_about(key_of[15], (2, L), 0.2, 3.0, (), jnp.float32),
        "w_self": scatter_about(key_of[16], (2, L, H), L ** -0.5, 0.25, ((2, 4),)),
        "w_agg": scatter_about(key_of[17], (2, L, H), L ** -0.5, 0.25, ((2, 4),)),
        "b_node": scatter_about(key_of[18], (2, H), 1.0, 6.0, ((1, 4),), jnp.float32),
        "w_node_out": scatter_about(key_of[19], (2, H, L), H ** -0.5, 0.25, ((1, 4),)),
        "b_node_out": scatter_about(key_of[20], (2, L), 0.5, 6.0, (), jnp.float32),
        "norm_gain": jnp.clip(1.0 + 0.18 * jax.random.normal(key_of[21], (2, L), jnp.float32), 0.1, 1.9),
        "norm_shift": scatter_about(key_of[22], (2, L), 0.5, 6.0, (), jnp.float32),
    }


def swish_unit(value):
    return value * jax.nn.sigmoid(value)

def to_bfloat(value):
    return lax.optimization_barrier(value.astype(jnp.bfloat16)).astype(jnp.float32)

def layer_norm(value, gain, shift):
    center = value - lax.optimization_barrier(jnp.mean(value, axis=-1, keepdims=True))
    spread = lax.optimization_barrier(jnp.mean(center * center, axis=-1, keepdims=True))
    return center * lax.rsqrt(spread + 1e-05) * gain + shift

def block_sum(left, right):
    width = left.shape[1] // N_FEAT
    left_blocks = left.reshape(left.shape[0], N_FEAT, width).astype(jnp.float32)
    right_blocks = right.reshape(N_FEAT, width, right.shape[1]).astype(jnp.float32)
    pieces = jnp.einsum('mfh,fhl->fml', left_blocks, right_blocks)
    return lax.optimization_barrier(jnp.sum(to_bfloat(pieces), axis=0))

def edge_hidden(send_rows, recv_proj, receivers, features, w_feat, bias):
    summed = send_rows.astype(jnp.float32) + recv_proj[jnp.maximum(receivers, 0)]
    summed = summed + jnp.einsum('ke,kh->eh', features, w_feat, precision=lax.Precision.HIGHEST) + bias
    hidden = to_bfloat(swish_unit(summed))
    targets = jnp.where(receivers >= 0, receivers, M_DEV)
    totals = jax.ops.segment_sum(hidden, targets, M_DEV + 1)[:M_DEV]
    counts = jax.ops.segment_sum(jnp.ones(receivers.shape, jnp.float32), targets, M_DEV + 1)[:M_DEV]
    return (totals, counts)

def node_step(latent, totals, counts, layer, w_edge_out, b_edge_out, w_self, w_agg, b_node, w_node_out, b_node_out, norm_gain, norm_shift):
    summed = totals.astype(jnp.bfloat16)
    gathered = block_sum(summed, w_edge_out[layer]) + counts[:, None] * b_edge_out[layer]
    preact = jnp.dot(latent, w_self[layer], preferred_element_type=jnp.float32)
    preact = preact + jnp.dot(gathered.astype(jnp.bfloat16), w_agg[layer], preferred_element_type=jnp.float32) + b_node[layer]
    hidden = swish_unit(preact).astype(jnp.bfloat16)
    update = block_sum(hidden, w_node_out[layer]) + b_node_out[layer]
    return (latent.astype(jnp.float32) + layer_norm(update, norm_gain[layer], norm_shift[layer])).astype(jnp.bfloat16)

def reference(grid_latent, mesh_latent, send_tiles, g2m_sender, g2m_receiver, g2m_feature, m2m_table, m2m_sender, m2m_receiver, m2m_feature, w_send, w_recv, w_edge_feat, b_edge, w_edge_out, b_edge_out, w_self, w_agg, b_node, w_node_out, b_node_out, norm_gain, norm_shift):
    node_weights = (w_edge_out, b_edge_out, w_self, w_agg, b_node, w_node_out, b_node_out, norm_gain, norm_shift)
    grid_proj = jnp.dot(grid_latent, w_send[0], preferred_element_type=jnp.float32).astype(jnp.bfloat16)
    mesh_proj = jnp.dot(mesh_latent, w_recv[0], preferred_element_type=jnp.float32)
    regions = jnp.arange(N_REGION, dtype=jnp.int32)

    def encode(region):
        senders = lax.dynamic_slice_in_dim(g2m_sender, region * G2M_DEV, G2M_DEV)
        receivers = lax.dynamic_slice_in_dim(g2m_receiver, region * G2M_DEV, G2M_DEV)
        features = lax.dynamic_slice_in_dim(g2m_feature, region * G2M_DEV, G2M_DEV, 1)
        source = senders // (CAP * TILE)
        slot_index = senders // TILE % CAP
        tile_index = send_tiles[source, region, slot_index]
        index = source * G_DEV + jnp.maximum(tile_index, 0) * TILE + senders % TILE
        rows = jnp.where((tile_index >= 0)[:, None], grid_proj[index], jnp.zeros((), jnp.bfloat16))
        latent = lax.dynamic_slice_in_dim(mesh_latent, region * M_DEV, M_DEV)
        recv_rows = lax.dynamic_slice_in_dim(mesh_proj, region * M_DEV, M_DEV)
        totals, counts = edge_hidden(rows, recv_rows, receivers, features, w_edge_feat[0], b_edge[0])
        return node_step(latent, totals, counts, 0, *node_weights)
    encoded = lax.map(encode, regions).reshape(MESH, L)
    mesh_send = jnp.dot(encoded, w_send[1], preferred_element_type=jnp.float32).astype(jnp.bfloat16)
    mesh_proj2 = jnp.dot(encoded, w_recv[1], preferred_element_type=jnp.float32)

    def process(region):
        senders = lax.dynamic_slice_in_dim(m2m_sender, region * M2M_DEV, M2M_DEV)
        receivers = lax.dynamic_slice_in_dim(m2m_receiver, region * M2M_DEV, M2M_DEV)
        features = lax.dynamic_slice_in_dim(m2m_feature, region * M2M_DEV, M2M_DEV, 1)
        source = senders // MCAP
        row_index = m2m_table[region, source, senders % MCAP]
        index = source * M_DEV + jnp.maximum(row_index, 0)
        rows = jnp.where((row_index >= 0)[:, None], mesh_send[index], jnp.zeros((), jnp.bfloat16))
        latent = lax.dynamic_slice_in_dim(encoded, region * M_DEV, M_DEV)
        recv_rows = lax.dynamic_slice_in_dim(mesh_proj2, region * M_DEV, M_DEV)
        totals, counts = edge_hidden(rows, recv_rows, receivers, features, w_edge_feat[1], b_edge[1])
        return node_step(latent, totals, counts, 1, *node_weights)
    processed = lax.map(process, regions).reshape(MESH, L)
    return (encoded, processed)
```

```python
import functools

import jax
import jax.numpy as jnp
from jax import lax
from jax.experimental import pallas as pl
from jax.experimental.pallas import tpu as pltpu
from jax.sharding import PartitionSpec as P

TILE = 128


def swish_unit(value):
    return value * jax.nn.sigmoid(value)


def layer_norm(value, gain, shift):
    center = value - jnp.mean(value, axis=-1, keepdims=True)
    spread = jnp.mean(center * center, axis=-1, keepdims=True)
    return center * lax.rsqrt(spread + 1e-05) * gain + shift


def select_rows(indices, table):
    picks = (indices[:, None] == jnp.arange(table.shape[0], dtype=jnp.int32)[None, :]).astype(
        jnp.bfloat16
    )
    return jnp.dot(picks, table, preferred_element_type=jnp.float32).astype(jnp.bfloat16)


def edge_sums(lookup, senders, receivers, features, recv_proj, w_feat, bias):
    node_count = recv_proj.shape[0]
    edge_count = senders.shape[0]
    edge_block = min(2048, edge_count)
    hidden_width = lookup.shape[1]
    node_ids = jnp.arange(node_count, dtype=jnp.int32)[:, None]
    recv_high = recv_proj.astype(jnp.bfloat16)
    recv_low = (recv_proj - recv_high.astype(jnp.float32)).astype(jnp.bfloat16)
    recv_pair = jnp.concatenate([recv_high, recv_low], axis=1)

    def visit_block(state_pair, start):
        totals, counts = state_pair
        send_part = lax.dynamic_slice_in_dim(senders, start, edge_block)
        recv_part = lax.dynamic_slice_in_dim(receivers, start, edge_block)
        feat_part = lax.dynamic_slice_in_dim(features, start, edge_block, 1)
        member = (node_ids == recv_part[None, :]).astype(jnp.bfloat16)
        picked = lax.dot_general(
            member, recv_pair, (((0,), (0,)), ((), ())), preferred_element_type=jnp.float32
        )
        recv_rows = picked[:, :hidden_width] + picked[:, hidden_width:]
        summed = lookup[send_part].astype(jnp.float32) + recv_rows
        summed = (
            summed
            + jnp.einsum("ke,kh->eh", feat_part, w_feat, precision=lax.Precision.HIGHEST)
            + bias
        )
        hidden = swish_unit(summed).astype(jnp.bfloat16)
        totals = totals + jnp.dot(member, hidden, preferred_element_type=jnp.float32)
        counts = counts + jnp.sum(member.astype(jnp.float32), axis=1)
        return ((totals, counts), None)

    starts = jnp.arange(edge_count // edge_block, dtype=jnp.int32) * edge_block
    initial = (
        jnp.zeros((node_count, hidden_width), jnp.float32),
        jnp.zeros((node_count,), jnp.float32),
    )
    result, unused = lax.scan(visit_block, initial, starts)
    return result


def node_step(
    latent,
    totals,
    counts,
    layer,
    full_outs,
    w_edge_out,
    b_edge_out,
    w_self,
    w_agg,
    b_node,
    w_node_out,
    b_node_out,
    norm_gain,
    norm_shift,
):
    summed = totals.astype(jnp.bfloat16)
    partial_agg = jnp.dot(summed, w_edge_out[layer], preferred_element_type=jnp.float32)
    gathered = (
        lax.psum(partial_agg.astype(jnp.bfloat16), "feat").astype(jnp.float32)
        + counts[:, None] * b_edge_out[layer]
    )
    preact = jnp.dot(latent, w_self[layer], preferred_element_type=jnp.float32)
    preact = (
        preact
        + jnp.dot(gathered.astype(jnp.bfloat16), w_agg[layer], preferred_element_type=jnp.float32)
        + b_node[layer]
    )
    hidden = swish_unit(preact).astype(jnp.bfloat16)
    partial_update = jnp.dot(hidden, w_node_out[layer], preferred_element_type=jnp.float32)
    update = (
        lax.psum(partial_update.astype(jnp.bfloat16), "feat").astype(jnp.float32)
        + b_node_out[layer]
    )
    return (
        latent.astype(jnp.float32) + layer_norm(update, norm_gain[layer], norm_shift[layer])
    ).astype(jnp.bfloat16)


def per_device(
    grid_latent,
    mesh_latent,
    send_tiles,
    g2m_sender,
    g2m_receiver,
    g2m_feature,
    m2m_table,
    m2m_sender,
    m2m_receiver,
    m2m_feature,
    w_send,
    w_recv,
    w_edge_feat,
    b_edge,
    w_edge_out,
    b_edge_out,
    w_self,
    w_agg,
    b_node,
    w_node_out,
    b_node_out,
    norm_gain,
    norm_shift,
):
    full_outs = (w_edge_out, w_node_out)
    node_weights = (
        full_outs,
        w_edge_out,
        b_edge_out,
        w_self,
        w_agg,
        b_node,
        w_node_out,
        b_node_out,
        norm_gain,
        norm_shift,
    )
    regions = lax.axis_size("region")
    hidden_width = w_send.shape[2]
    grid_proj = jnp.dot(grid_latent, w_send[0], preferred_element_type=jnp.float32).astype(
        jnp.bfloat16
    )
    wanted = send_tiles[0]
    tile_table = grid_proj.reshape(-1, TILE * hidden_width)
    tiles = select_rows(wanted.reshape(-1), tile_table).reshape(regions, -1, TILE * hidden_width)
    arrived = lax.all_to_all(tiles, "region", split_axis=0, concat_axis=0, tiled=True)
    grid_lookup = arrived.reshape(-1, hidden_width)
    recv_first = jnp.dot(mesh_latent, w_recv[0], preferred_element_type=jnp.float32)
    totals, counts = edge_sums(
        grid_lookup, g2m_sender, g2m_receiver, g2m_feature, recv_first, w_edge_feat[0], b_edge[0]
    )
    encoded = node_step(mesh_latent, totals, counts, 0, *node_weights)
    mesh_send = jnp.dot(encoded, w_send[1], preferred_element_type=jnp.float32).astype(jnp.bfloat16)
    everything = lax.all_gather(mesh_send, "region", axis=0, tiled=True)
    wanted = m2m_table[0]
    capacity = wanted.shape[1]
    source = m2m_sender // capacity
    row_index = wanted[source, m2m_sender % capacity]
    mesh_index = source * mesh_latent.shape[0] + jnp.maximum(row_index, 0)
    recv_second = jnp.dot(encoded, w_recv[1], preferred_element_type=jnp.float32)
    totals, counts = edge_sums(
        everything, mesh_index, m2m_receiver, m2m_feature, recv_second, w_edge_feat[1], b_edge[1]
    )
    processed = node_step(encoded, totals, counts, 1, *node_weights)
    columns = mesh_latent.shape[1] // lax.axis_size("feat")
    first_column = lax.axis_index("feat") * columns
    return (
        lax.dynamic_slice_in_dim(encoded, first_column, columns, 1),
        lax.dynamic_slice_in_dim(processed, first_column, columns, 1),
    )


MESH = pl.DeviceIdType.MESH
BF = jnp.bfloat16
F32 = jnp.float32


def dot_dims(left, right, left_dim, right_dim):
    return lax.dot_general(
        left, right, (((left_dim,), (right_dim,)), ((), ())), preferred_element_type=F32
    )


def one_hot(row, count):
    ids = lax.broadcasted_iota(jnp.int32, (count, row.shape[1]), 0)
    return jnp.where(ids == row, 1.0, 0.0).astype(BF)


def swish_tanh(value):
    half = 0.5 * value
    return half + half * jnp.tanh(half)


def fused(
    regions, feats,
    grid_ref, mesh_ref, tiles_ref, gs_ref, gr_ref, gf_ref, mt_ref, ms_ref, mr_ref, mf_ref,
    w_send, w_recv, w_ef, b_edge, weo_ref, beo, wself_ref, wagg_ref, bnode_ref, wno_ref, bno,
    gain, shift,
    out_enc, out_proc,
    proj, stage, tab, table_all, recv_tab, acc, cols,
    weo, wno, wself, wagg, bnode, sum_stage, sum_all, cnt_stage, enc, stage2, tab2, fold2,
    proc_stage, proc_all,
    tile_send, tile_recv, id_send, id_recv, w_ssem, w_rsem, b_ssem, b_rsem, s_ssem, s_rsem,
    e_ssem, e_rsem, m_ssem, m_rsem, p_ssem, p_rsem,
):
    reg = lax.axis_index("region")
    ft = lax.axis_index("feat")
    width = w_send.shape[2]
    nodes = mesh_ref.shape[0]
    slots = tab.shape[2]
    rows = nodes // feats
    core = ft % 2
    across = (ft + 2) % feats
    partner = ft - core + (1 - core)

    barrier = pltpu.get_barrier_semaphore()
    for off in range(1, regions):
        pl.semaphore_signal(
            barrier, inc=1, device_id={"region": (reg + off) % regions}, device_id_type=MESH
        )
    for off in range(1, feats):
        pl.semaphore_signal(
            barrier, inc=1, device_id={"feat": (ft + off) % feats}, device_id_type=MESH
        )
    pl.semaphore_wait(barrier, regions + feats - 2)

    def remote(source, target, send, recv, axis, index):
        return pltpu.make_async_remote_copy(
            src_ref=source, dst_ref=target, send_sem=send, recv_sem=recv,
            device_id={axis: index}, device_id_type=MESH,
        )

    def to_peers(axis, me, count, source_of, target_of, send, recv):
        copies = []
        for off in range(1, count):
            peer = (me + off) % count
            copies.append(
                remote(source_of(peer), target_of(me), send.at[off - 1], recv.at[off - 1], axis, peer)
            )
        return copies

    id_copies = to_peers(
        "region", reg, regions, lambda p: mt_ref.at[0], lambda m: table_all.at[m], id_send, id_recv
    )
    bias_copies = to_peers(
        "feat", ft, feats, lambda p: bnode_ref, lambda m: bnode.at[m], b_ssem, b_rsem
    )
    kinds = ((weo_ref, weo), (wself_ref, wself), (wagg_ref, wagg), (wno_ref, wno))

    def weight_copies(layer, route):
        copies = []
        for kind, (own, full) in enumerate(kinds):
            slot = across if route == 2 else ft
            source = full.at[layer, slot] if route == 2 else own.at[layer]
            copies.append(
                remote(
                    source, full.at[layer, slot],
                    w_ssem.at[layer, route, kind], w_rsem.at[layer, route, kind],
                    "feat", across if route == 0 else partner,
                )
            )
        return copies

    first_hops = [[weight_copies(layer, route) for route in range(2)] for layer in range(2)]
    forwards = [weight_copies(layer, 2) for layer in range(2)]
    for copy in id_copies + bias_copies:
        copy.start()

    @pl.loop(0, grid_ref.shape[0] // 512)
    def project(step):
        block = dot_dims(w_send[0], grid_ref[pl.ds(step * 512, 512), :], 0, 1).astype(BF)
        for part in range(512 // TILE):
            proj[step * (512 // TILE) + part] = block[:, part * TILE : (part + 1) * TILE]

    cap = slots // TILE
    for target in range(regions):
        for slot in range(cap):
            tile = jnp.maximum(tiles_ref[0, target, slot], 0)
            stage[target, :, slot * TILE : (slot + 1) * TILE] = proj[tile]
    tile_copies = to_peers(
        "region", reg, regions, lambda p: stage.at[p], lambda m: tab.at[m], tile_send, tile_recv
    )
    for copy in tile_copies:
        copy.start()
    for layer in range(2):
        for route in range(2):
            for copy in first_hops[layer][route]:
                copy.start()
    tab[reg] = stage[reg]
    table_all[reg] = mt_ref[0]
    bnode[ft] = bnode_ref[...]
    for layer in range(2):
        for own, full in kinds:
            full[layer, ft] = own[layer]

    half_nodes = nodes // 2

    def set_receivers(layer, latent):
        base = jnp.concatenate(
            [w_ef[layer], b_edge[layer : layer + 1], jnp.zeros((3, width), F32)], axis=0
        )
        turned = jnp.concatenate([base] * (width // 8), axis=0).T
        cols[...] = turned
        table = dot_dims(w_recv[layer], latent, 0, 1) + turned[:, 4:5]
        table = table.astype(BF)
        recv_tab[0:width] = table[:, :half_nodes]
        recv_tab[width:] = table[:, half_nodes:]
        acc[...] = jnp.zeros_like(acc)

    def edge_block(at, size, s_ref, r_ref, f_ref, table, shift_by):
        here = pl.ds(pl.multiple_of(at, size), size)
        send = s_ref[:, here]
        recv = r_ref[:, here]
        upper = recv >= half_nodes
        low = jnp.where(upper, recv - half_nodes, recv)
        picks = one_hot(low, half_nodes)
        found = jnp.dot(recv_tab[...], picks, preferred_element_type=F32)
        value = jnp.where(upper, found[width:], found[:width])
        source = send >> shift_by
        local = send & ((1 << shift_by) - 1)
        found = jnp.dot(table, one_hot(local, 1 << shift_by), preferred_element_type=F32)
        chosen = found[:width]
        for part in range(1, table.shape[0] // width):
            chosen = jnp.where(source == part, found[part * width : (part + 1) * width], chosen)
        value = value + chosen
        for k in range(4):
            value = value + cols[:, k : k + 1] * f_ref[k : k + 1, here]
        hidden = swish_tanh(value)
        ids = lax.broadcasted_iota(jnp.int32, (16, size), 0)
        side = jnp.where(upper, 1, 0)
        spread = jnp.concatenate(
            [
                jnp.where(upper, 0.0, hidden).astype(BF),
                jnp.where(upper, hidden, 0.0).astype(BF),
                jnp.where(ids == side, 1.0, 0.0).astype(BF),
            ],
            axis=0,
        )
        acc[...] += dot_dims(spread, picks, 1, 1)

    def share_sums(layer):
        for owner in range(feats):
            side = (owner * rows) // half_nodes
            lane = (owner * rows) % half_nodes
            sum_stage[layer, owner] = acc[
                side * width : (side + 1) * width, lane : lane + rows
            ].astype(BF)
            cnt_stage[owner] = acc[2 * width + side : 2 * width + side + 1, lane : lane + rows]
        copies = to_peers(
            "feat", ft, feats, lambda p: sum_stage.at[layer, p], lambda m: sum_all.at[layer, m],
            s_ssem.at[layer], s_rsem.at[layer],
        )
        for copy in copies:
            copy.start()
        sum_all[layer, ft] = sum_stage[layer, ft]
        return copies

    def node_rows(layer, latent):
        sums = sum_all[layer].reshape(feats * width, rows)
        agg = dot_dims(sums, weo[layer].reshape(feats * width, -1), 0, 0)
        count = jnp.broadcast_to(cnt_stage[ft], (rows, rows)).T
        agg = agg + jnp.concatenate([count] * (agg.shape[1] // rows), axis=1) * beo[layer : layer + 1]
        agg = agg.astype(BF)
        update = bno[layer : layer + 1]
        for part in range(feats):
            pre = jnp.dot(latent, wself[layer, part], preferred_element_type=F32)
            pre = pre + jnp.dot(agg, wagg[layer, part], preferred_element_type=F32)
            hidden = swish_tanh(pre + bnode[part, layer : layer + 1]).astype(BF)
            update = update + jnp.dot(hidden, wno[layer, part], preferred_element_type=F32)
        normed = layer_norm(update, gain[layer : layer + 1], shift[layer : layer + 1])
        return (latent.astype(F32) + normed).astype(BF)

    set_receivers(0, mesh_ref[...])
    for copy in tile_copies:
        copy.wait()
    size = 512
    steps = gs_ref.shape[1] // size
    shift_first = slots.bit_length() - 1

    @pl.loop(0, steps // 2)
    def first_half(step):
        edge_block(step * size, size, gs_ref, gr_ref, gf_ref, tab[...].reshape(regions * width, slots), shift_first)

    for copy in first_hops[0][0]:
        copy.wait_recv()
    for copy in forwards[0]:
        copy.start()

    @pl.loop(steps // 2, steps)
    def second_half(step):
        edge_block(step * size, size, gs_ref, gr_ref, gf_ref, tab[...].reshape(regions * width, slots), shift_first)

    sums = share_sums(0)
    for copy in first_hops[0][1] + forwards[0] + sums + bias_copies:
        copy.wait()
    for copy in first_hops[1][0]:
        copy.wait_recv()
    for copy in forwards[1]:
        copy.start()
    mine = pl.ds(pl.multiple_of(ft * rows, rows), rows)
    enc[ft] = node_rows(0, mesh_ref[mine, :])
    enc_copies = to_peers(
        "feat", ft, feats, lambda p: enc.at[ft], lambda m: enc.at[m], e_ssem, e_rsem
    )
    for copy in enc_copies:
        copy.start()
    for copy in id_copies + enc_copies:
        copy.wait()
    whole = enc[...].reshape(nodes, -1)
    sent = dot_dims(w_send[1], whole, 0, 1).astype(BF)
    for target in range(regions):
        wanted = table_all[target, pl.ds(reg, 1), :]
        stage2[target] = jnp.dot(sent, one_hot(wanted, nodes), preferred_element_type=F32).astype(BF)
    row_copies = to_peers(
        "region", reg, regions, lambda p: stage2.at[p], lambda m: tab2.at[m], m_ssem, m_rsem
    )
    for copy in row_copies:
        copy.start()
    tab2[reg] = stage2[reg]
    set_receivers(1, whole)
    for owner in range(feats):
        out_enc[owner * rows : (owner + 1) * rows, :] = enc[owner, :, pl.ds(pl.multiple_of(ft * width, width), width)]
    for copy in row_copies:
        copy.wait()
    mcap = tab2.shape[2]
    for part in range(regions):
        fold2[
            (part // 2) * width : (part // 2 + 1) * width, (part % 2) * mcap : (part % 2 + 1) * mcap
        ] = tab2[part]
    shift_second = (2 * mcap).bit_length() - 1

    @pl.loop(0, ms_ref.shape[1] // size)
    def mesh_steps(step):
        edge_block(step * size, size, ms_ref, mr_ref, mf_ref, fold2[...], shift_second)

    sums = share_sums(1)
    for copy in first_hops[1][1] + forwards[1] + sums:
        copy.wait()
    for layer in range(2):
        for copy in first_hops[layer][0]:
            copy.wait_send()
    result = node_rows(1, enc[ft])
    for owner in range(feats):
        proc_stage[owner] = result[:, owner * width : (owner + 1) * width]
    proc_copies = to_peers(
        "feat", ft, feats, lambda p: proc_stage.at[p], lambda m: proc_all.at[m], p_ssem, p_rsem
    )
    for copy in proc_copies:
        copy.start()
    proc_all[ft] = proc_stage[ft]
    for copy in proc_copies:
        copy.wait()
    out_proc[...] = proc_all[...].reshape(nodes, width)


def fused_device(regions, feats, *args):
    (grid_latent, mesh_latent, send_tiles, gs, gr, gf, mt, ms, mr, mf, w_send) = args[:11]
    nodes, latent = mesh_latent.shape
    width = w_send.shape[2]
    slots = send_tiles.shape[2] * TILE
    mcap = mt.shape[2]
    rows = nodes // feats
    args = list(args)
    for at in (3, 4, 7, 8):
        args[at] = args[at].reshape(1, -1)
    specs = [pl.BlockSpec(memory_space=pltpu.VMEM)] * len(args)
    specs[2] = pl.BlockSpec(memory_space=pltpu.SMEM)
    dma = pltpu.SemaphoreType.DMA
    vm = pltpu.VMEM
    return pl.pallas_call(
        functools.partial(fused, regions, feats),
        out_shape=(jax.ShapeDtypeStruct((nodes, width), BF),) * 2,
        in_specs=specs,
        out_specs=(pl.BlockSpec(memory_space=pltpu.VMEM),) * 2,
        scratch_shapes=[
            vm((grid_latent.shape[0] // TILE, width, TILE), BF),
            vm((regions, width, slots), BF),
            vm((regions, width, slots), BF),
            vm((regions, regions, mcap), jnp.int32),
            vm((2 * width, nodes // 2), BF),
            vm((2 * width + 16, nodes // 2), F32),
            vm((width, width), F32),
            vm((2, feats, width, latent), BF),
            vm((2, feats, width, latent), BF),
            vm((2, feats, latent, width), BF),
            vm((2, feats, latent, width), BF),
            vm((feats, 2, width), F32),
            vm((2, feats, width, rows), BF),
            vm((2, feats, width, rows), BF),
            vm((feats, 1, rows), F32),
            vm((feats, rows, latent), BF),
            vm((regions, width, mcap), BF),
            vm((regions, width, mcap), BF),
            vm((regions // 2 * width, 2 * mcap), BF),
            vm((feats, rows, width), BF),
            vm((feats, rows, width), BF),
            dma((regions - 1,)), dma((regions - 1,)),
            dma((regions - 1,)), dma((regions - 1,)),
            dma((2, 3, 4)), dma((2, 3, 4)),
            dma((feats - 1,)), dma((feats - 1,)),
            dma((2, feats - 1)), dma((2, feats - 1)),
            dma((feats - 1,)), dma((feats - 1,)),
            dma((regions - 1,)), dma((regions - 1,)),
            dma((feats - 1,)), dma((feats - 1,)),
        ],
        compiler_params=pltpu.CompilerParams(
            collective_id=0, has_side_effects=True, vmem_limit_bytes=48 << 20
        ),
    )(*args)


def pick_form(regions, feats, *args):
    width = args[10].shape[2]
    rows = args[1].shape[0] // feats
    if feats == 4 and width == 128 and rows == 128 and regions % 2 == 0 and regions <= 8:
        return fused_device(regions, feats, *args)
    return per_device(*args)


def solution(mesh):
    return jax.shard_map(
        functools.partial(pick_form, mesh.shape["region"], mesh.shape["feat"]),
        mesh=mesh,
        in_specs=(
            P(("parts", "region"), None),
            P(("parts", "region"), None),
            P(("parts", "region"), None, None),
            P(("parts", "region")),
            P(("parts", "region")),
            P(None, ("parts", "region")),
            P(("parts", "region"), None, None),
            P(("parts", "region")),
            P(("parts", "region")),
            P(None, ("parts", "region")),
            P(None, None, "feat"),
            P(None, None, "feat"),
            P(None, None, "feat"),
            P(None, "feat"),
            P(None, "feat", None),
            P(),
            P(None, None, "feat"),
            P(None, None, "feat"),
            P(None, "feat"),
            P(None, "feat", None),
            P(),
            P(),
            P(),
        ),
        out_specs=(P(("parts", "region"), "feat"), P(("parts", "region"), "feat")),
        check_vma=False,
    )
```

```python
import functools

import jax
import jax.numpy as jnp
from jax import lax
from jax.experimental import pallas as pl
from jax.experimental.pallas import tpu as pltpu
from jax.sharding import PartitionSpec as P

TILE = 128


def swish_unit(value):
    return value * jax.nn.sigmoid(value)


def layer_norm(value, gain, shift):
    center = value - jnp.mean(value, axis=-1, keepdims=True)
    spread = jnp.mean(center * center, axis=-1, keepdims=True)
    return center * lax.rsqrt(spread + 1e-05) * gain + shift


def select_rows(indices, table):
    picks = (indices[:, None] == jnp.arange(table.shape[0], dtype=jnp.int32)[None, :]).astype(
        jnp.bfloat16
    )
    return jnp.dot(picks, table, preferred_element_type=jnp.float32).astype(jnp.bfloat16)


def edge_sums(lookup, senders, receivers, features, recv_proj, w_feat, bias):
    node_count = recv_proj.shape[0]
    edge_count = senders.shape[0]
    edge_block = min(2048, edge_count)
    hidden_width = lookup.shape[1]
    node_ids = jnp.arange(node_count, dtype=jnp.int32)[:, None]
    recv_high = recv_proj.astype(jnp.bfloat16)
    recv_low = (recv_proj - recv_high.astype(jnp.float32)).astype(jnp.bfloat16)
    recv_pair = jnp.concatenate([recv_high, recv_low], axis=1)

    def visit_block(state_pair, start):
        totals, counts = state_pair
        send_part = lax.dynamic_slice_in_dim(senders, start, edge_block)
        recv_part = lax.dynamic_slice_in_dim(receivers, start, edge_block)
        feat_part = lax.dynamic_slice_in_dim(features, start, edge_block, 1)
        member = (node_ids == recv_part[None, :]).astype(jnp.bfloat16)
        picked = lax.dot_general(
            member, recv_pair, (((0,), (0,)), ((), ())), preferred_element_type=jnp.float32
        )
        recv_rows = picked[:, :hidden_width] + picked[:, hidden_width:]
        summed = lookup[send_part].astype(jnp.float32) + recv_rows
        summed = (
            summed
            + jnp.einsum("ke,kh->eh", feat_part, w_feat, precision=lax.Precision.HIGHEST)
            + bias
        )
        hidden = swish_unit(summed).astype(jnp.bfloat16)
        totals = totals + jnp.dot(member, hidden, preferred_element_type=jnp.float32)
        counts = counts + jnp.sum(member.astype(jnp.float32), axis=1)
        return ((totals, counts), None)

    starts = jnp.arange(edge_count // edge_block, dtype=jnp.int32) * edge_block
    initial = (
        jnp.zeros((node_count, hidden_width), jnp.float32),
        jnp.zeros((node_count,), jnp.float32),
    )
    result, unused = lax.scan(visit_block, initial, starts)
    return result


def node_step(
    latent,
    totals,
    counts,
    layer,
    full_outs,
    w_edge_out,
    b_edge_out,
    w_self,
    w_agg,
    b_node,
    w_node_out,
    b_node_out,
    norm_gain,
    norm_shift,
):
    summed = totals.astype(jnp.bfloat16)
    partial_agg = jnp.dot(summed, w_edge_out[layer], preferred_element_type=jnp.float32)
    gathered = (
        lax.psum(partial_agg.astype(jnp.bfloat16), "feat").astype(jnp.float32)
        + counts[:, None] * b_edge_out[layer]
    )
    preact = jnp.dot(latent, w_self[layer], preferred_element_type=jnp.float32)
    preact = (
        preact
        + jnp.dot(gathered.astype(jnp.bfloat16), w_agg[layer], preferred_element_type=jnp.float32)
        + b_node[layer]
    )
    hidden = swish_unit(preact).astype(jnp.bfloat16)
    partial_update = jnp.dot(hidden, w_node_out[layer], preferred_element_type=jnp.float32)
    update = (
        lax.psum(partial_update.astype(jnp.bfloat16), "feat").astype(jnp.float32)
        + b_node_out[layer]
    )
    return (
        latent.astype(jnp.float32) + layer_norm(update, norm_gain[layer], norm_shift[layer])
    ).astype(jnp.bfloat16)


def per_device(
    grid_latent,
    mesh_latent,
    send_tiles,
    g2m_sender,
    g2m_receiver,
    g2m_feature,
    m2m_table,
    m2m_sender,
    m2m_receiver,
    m2m_feature,
    w_send,
    w_recv,
    w_edge_feat,
    b_edge,
    w_edge_out,
    b_edge_out,
    w_self,
    w_agg,
    b_node,
    w_node_out,
    b_node_out,
    norm_gain,
    norm_shift,
):
    full_outs = (w_edge_out, w_node_out)
    node_weights = (
        full_outs,
        w_edge_out,
        b_edge_out,
        w_self,
        w_agg,
        b_node,
        w_node_out,
        b_node_out,
        norm_gain,
        norm_shift,
    )
    regions = lax.axis_size("region")
    hidden_width = w_send.shape[2]
    grid_proj = jnp.dot(grid_latent, w_send[0], preferred_element_type=jnp.float32).astype(
        jnp.bfloat16
    )
    wanted = send_tiles[0]
    tile_table = grid_proj.reshape(-1, TILE * hidden_width)
    tiles = select_rows(wanted.reshape(-1), tile_table).reshape(regions, -1, TILE * hidden_width)
    arrived = lax.all_to_all(tiles, "region", split_axis=0, concat_axis=0, tiled=True)
    grid_lookup = arrived.reshape(-1, hidden_width)
    recv_first = jnp.dot(mesh_latent, w_recv[0], preferred_element_type=jnp.float32)
    totals, counts = edge_sums(
        grid_lookup, g2m_sender, g2m_receiver, g2m_feature, recv_first, w_edge_feat[0], b_edge[0]
    )
    encoded = node_step(mesh_latent, totals, counts, 0, *node_weights)
    mesh_send = jnp.dot(encoded, w_send[1], preferred_element_type=jnp.float32).astype(jnp.bfloat16)
    everything = lax.all_gather(mesh_send, "region", axis=0, tiled=True)
    wanted = m2m_table[0]
    capacity = wanted.shape[1]
    source = m2m_sender // capacity
    row_index = wanted[source, m2m_sender % capacity]
    mesh_index = source * mesh_latent.shape[0] + jnp.maximum(row_index, 0)
    recv_second = jnp.dot(encoded, w_recv[1], preferred_element_type=jnp.float32)
    totals, counts = edge_sums(
        everything, mesh_index, m2m_receiver, m2m_feature, recv_second, w_edge_feat[1], b_edge[1]
    )
    processed = node_step(encoded, totals, counts, 1, *node_weights)
    columns = mesh_latent.shape[1] // lax.axis_size("feat")
    first_column = lax.axis_index("feat") * columns
    return (
        lax.dynamic_slice_in_dim(encoded, first_column, columns, 1),
        lax.dynamic_slice_in_dim(processed, first_column, columns, 1),
    )


MESH = pl.DeviceIdType.MESH
BF = jnp.bfloat16
EDGE_BLOCK = 2048
F32 = jnp.float32


def dot_dims(left, right, left_dim, right_dim):
    return lax.dot_general(
        left, right, (((left_dim,), (right_dim,)), ((), ())), preferred_element_type=F32
    )


def one_hot(row, count):
    ids = lax.broadcasted_iota(jnp.int32, (count, row.shape[1]), 0)
    return jnp.where(ids == row, 1.0, 0.0).astype(BF)


def swish_tanh(value):
    half = 0.5 * value
    return half + half * jnp.tanh(half)


def fused(
    regions, feats,
    grid_hbm, mesh_hbm, tiles_ref, gs_hbm, gr_hbm, gf_hbm, mt_hbm, ms_hbm, mr_hbm, mf_hbm,
    w_send_hbm, w_recv_hbm, w_ef_hbm, b_edge_hbm, weo_ref, beo_hbm, wself_ref, wagg_ref, bnode_hbm,
    wno_ref, bno_hbm, gain_hbm, shift_hbm,
    out_enc, out_proc,
    proj, stage, tab, table_all, recv_tab, acc, cols,
    weo, wno, wself, wagg, bnode, sum_stage, sum_all, cnt_stage, enc, stage2, tab2, fold2,
    proc_stage, proc_all, send_picks, recv_picks, partial_sum,
    grid_ref, w_send, mesh_ref, w_recv, w_ef, b_edge, gs_ref, gr_ref, gf_ref, mt_ref, ms_ref,
    mr_ref, mf_ref, beo, bnode_ref, bno, gain, shift, in_sem, own_sem,
    tile_send, tile_recv, id_send, id_recv, w_ssem, w_rsem, b_ssem, b_rsem, s_ssem, s_rsem,
    e_ssem, e_rsem, m_ssem, m_rsem, p_ssem, p_rsem,
):
    reg = lax.axis_index("region")
    ft = lax.axis_index("feat")
    width = w_send.shape[2]
    nodes = mesh_ref.shape[0]
    slots = tab.shape[2]
    rows = nodes // feats
    core = ft % 2
    across = (ft + 2) % feats
    partner = ft - core + (1 - core)

    loads = [
        pltpu.make_async_copy(source, target, in_sem.at[at])
        for at, (source, target) in enumerate(
            (
                (w_send_hbm, w_send), (grid_hbm, grid_ref), (mesh_hbm, mesh_ref),
                (w_recv_hbm, w_recv), (w_ef_hbm, w_ef), (b_edge_hbm, b_edge), (gs_hbm, gs_ref),
                (gr_hbm, gr_ref), (gf_hbm, gf_ref), (mt_hbm, mt_ref), (bnode_hbm, bnode_ref),
                (ms_hbm, ms_ref), (mr_hbm, mr_ref), (mf_hbm, mf_ref), (beo_hbm, beo),
                (bno_hbm, bno), (gain_hbm, gain), (shift_hbm, shift),
            )
        )
    ]
    for load in loads:
        load.start()
    barrier = pltpu.get_barrier_semaphore()
    for off in range(1, regions):
        pl.semaphore_signal(
            barrier, inc=1, device_id={"region": (reg + off) % regions}, device_id_type=MESH
        )
    for off in range(1, feats):
        pl.semaphore_signal(
            barrier, inc=1, device_id={"feat": (ft + off) % feats}, device_id_type=MESH
        )
    pl.semaphore_wait(barrier, regions + feats - 2)

    def remote(source, target, send, recv, axis, index):
        return pltpu.make_async_remote_copy(
            src_ref=source, dst_ref=target, send_sem=send, recv_sem=recv,
            device_id={axis: index}, device_id_type=MESH,
        )

    def to_peers(axis, me, count, source_of, target_of, send, recv):
        copies = []
        for off in range(1, count):
            peer = (me + off) % count
            copies.append(
                remote(source_of(peer), target_of(me), send.at[off - 1], recv.at[off - 1], axis, peer)
            )
        return copies

    id_copies = to_peers(
        "region", reg, regions, lambda p: mt_ref.at[0], lambda m: table_all.at[m], id_send, id_recv
    )
    bias_copies = to_peers(
        "feat", ft, feats, lambda p: bnode_ref, lambda m: bnode.at[m], b_ssem, b_rsem
    )
    kinds = ((weo_ref, weo), (wself_ref, wself), (wagg_ref, wagg), (wno_ref, wno))

    def weight_copies(layer, route):
        copies = []
        for kind, (own, full) in enumerate(kinds):
            slot = across if route == 2 else ft
            source = full.at[layer, slot] if route == 2 else own.at[layer]
            copies.append(
                remote(
                    source, full.at[layer, slot],
                    w_ssem.at[layer, route, kind], w_rsem.at[layer, route, kind],
                    "feat", across if route == 0 else partner,
                )
            )
        return copies

    first_hops = [[weight_copies(layer, route) for route in range(2)] for layer in range(2)]
    forwards = [weight_copies(layer, 2) for layer in range(2)]
    for route in range(2):
        for copy in first_hops[0][route]:
            copy.start()
    for load in loads[:2]:
        load.wait()

    @pl.loop(0, grid_ref.shape[0] // 512)
    def project(step):
        block = dot_dims(w_send[0], grid_ref[pl.ds(step * 512, 512), :], 0, 1).astype(BF)
        for part in range(512 // TILE):
            proj[step * (512 // TILE) + part] = block[:, part * TILE : (part + 1) * TILE]

    cap = slots // TILE
    for target in range(regions):
        for slot in range(cap):
            tile = jnp.maximum(tiles_ref[0, target, slot], 0)
            stage[target, :, slot * TILE : (slot + 1) * TILE] = proj[tile]
    tile_copies = to_peers(
        "region", reg, regions, lambda p: stage.at[p], lambda m: tab.at[m], tile_send, tile_recv
    )
    for copy in tile_copies:
        copy.start()
    for load in loads[2:]:
        load.wait()
    for copy in id_copies + bias_copies:
        copy.start()
    for route in range(2):
        for copy in first_hops[1][route]:
            copy.start()
    keeps = [
        pltpu.make_async_copy(own.at[layer], full.at[layer, ft], own_sem.at[layer, kind])
        for layer in range(2)
        for kind, (own, full) in enumerate(kinds)
    ]
    for copy in keeps:
        copy.start()
    tab[reg] = stage[reg]
    table_all[reg] = mt_ref[0]
    bnode[ft] = bnode_ref[...]

    half_nodes = nodes // 2

    def set_receivers(layer, latent):
        base = jnp.concatenate(
            [w_ef[layer], b_edge[layer : layer + 1], jnp.zeros((3, width), F32)], axis=0
        )
        turned = jnp.concatenate([base] * (width // 8), axis=0).T
        cols[...] = turned
        table = dot_dims(w_recv[layer], latent, 0, 1) + turned[:, 4:5]
        table = table.astype(BF)
        recv_tab[0:width] = table[:, :half_nodes]
        recv_tab[width:] = table[:, half_nodes:]
        acc[...] = jnp.zeros_like(acc)

    def pick_edges(step, s_ref, r_ref, shift_by):
        here = pl.ds(pl.multiple_of(step * size, size), size)
        recv = r_ref[:, here]
        low = jnp.where(recv >= half_nodes, recv - half_nodes, recv)
        recv_picks[step] = one_hot(low, half_nodes)
        local = s_ref[:, here] & ((1 << shift_by) - 1)
        send_picks[step, 0 : 1 << shift_by] = one_hot(local, 1 << shift_by)

    def start_edges(step, r_ref, f_ref):
        here = pl.ds(pl.multiple_of(step * size, size), size)
        found = jnp.dot(recv_tab[...], recv_picks[step], preferred_element_type=F32)
        value = jnp.where(r_ref[:, here] >= half_nodes, found[width:], found[:width])
        for k in range(4):
            value = value + cols[:, k : k + 1] * f_ref[k : k + 1, here]
        partial_sum[step] = value

    def finish_edges(step, s_ref, r_ref, table, shift_by):
        here = pl.ds(pl.multiple_of(step * size, size), size)
        source = s_ref[:, here] >> shift_by
        upper = r_ref[:, here] >= half_nodes
        found = jnp.dot(
            table, send_picks[step, 0 : 1 << shift_by], preferred_element_type=F32
        )
        chosen = found[:width]
        for part in range(1, table.shape[0] // width):
            chosen = jnp.where(source == part, found[part * width : (part + 1) * width], chosen)
        hidden = swish_tanh(partial_sum[step] + chosen)
        ids = lax.broadcasted_iota(jnp.int32, (16, size), 0)
        side = jnp.where(upper, 1, 0)
        spread = jnp.concatenate(
            [
                jnp.where(upper, 0.0, hidden).astype(BF),
                jnp.where(upper, hidden, 0.0).astype(BF),
                jnp.where(ids == side, 1.0, 0.0).astype(BF),
            ],
            axis=0,
        )
        acc[...] += dot_dims(spread, recv_picks[step], 1, 1)

    def share_sums(layer):
        for owner in range(feats):
            side = (owner * rows) // half_nodes
            lane = (owner * rows) % half_nodes
            sum_stage[layer, owner] = acc[
                side * width : (side + 1) * width, lane : lane + rows
            ].astype(BF)
            cnt_stage[owner] = acc[2 * width + side : 2 * width + side + 1, lane : lane + rows]
        copies = to_peers(
            "feat", ft, feats, lambda p: sum_stage.at[layer, p], lambda m: sum_all.at[layer, m],
            s_ssem.at[layer], s_rsem.at[layer],
        )
        for copy in copies:
            copy.start()
        sum_all[layer, ft] = sum_stage[layer, ft]
        return copies

    def node_rows(layer, latent):
        sums = sum_all[layer].reshape(feats * width, rows)
        agg = dot_dims(sums, weo[layer].reshape(feats * width, -1), 0, 0)
        count = jnp.broadcast_to(cnt_stage[ft], (rows, rows)).T
        agg = agg + jnp.concatenate([count] * (agg.shape[1] // rows), axis=1) * beo[layer : layer + 1]
        agg = agg.astype(BF)
        update = bno[layer : layer + 1]
        for part in range(feats):
            pre = jnp.dot(latent, wself[layer, part], preferred_element_type=F32)
            pre = pre + jnp.dot(agg, wagg[layer, part], preferred_element_type=F32)
            hidden = swish_tanh(pre + bnode[part, layer : layer + 1]).astype(BF)
            update = update + jnp.dot(hidden, wno[layer, part], preferred_element_type=F32)
        normed = layer_norm(update, gain[layer : layer + 1], shift[layer : layer + 1])
        return (latent.astype(F32) + normed).astype(BF)

    set_receivers(0, mesh_ref[...])
    size = send_picks.shape[2]
    steps = gs_ref.shape[1] // size
    shift_first = slots.bit_length() - 1

    @pl.loop(0, steps)
    def begin(step):
        pick_edges(step, gs_ref, gr_ref, shift_first)
        start_edges(step, gr_ref, gf_ref)

    for copy in tile_copies:
        copy.wait()
    for copy in first_hops[0][0]:
        copy.wait_recv()
    for copy in forwards[0]:
        copy.start()

    @pl.loop(0, steps)
    def finish(step):
        table = tab[...].reshape(regions * width, slots)
        finish_edges(step, gs_ref, gr_ref, table, shift_first)

    sums = share_sums(0)
    for copy in keeps + first_hops[0][1] + forwards[0] + sums + bias_copies:
        copy.wait()
    for copy in first_hops[1][0]:
        copy.wait_recv()
    for copy in forwards[1]:
        copy.start()
    mine = pl.ds(pl.multiple_of(ft * rows, rows), rows)
    enc[ft] = node_rows(0, mesh_ref[mine, :])
    enc_copies = to_peers(
        "feat", ft, feats, lambda p: enc.at[ft], lambda m: enc.at[m], e_ssem, e_rsem
    )
    for copy in enc_copies:
        copy.start()
    mcap = tab2.shape[2]
    shift_second = (2 * mcap).bit_length() - 1
    mesh_steps = ms_ref.shape[1] // size

    @pl.loop(0, mesh_steps)
    def pick_mesh(step):
        pick_edges(step, ms_ref, mr_ref, shift_second)

    for copy in id_copies + enc_copies:
        copy.wait()
    whole = enc[...].reshape(nodes, -1)
    sent = dot_dims(w_send[1], whole, 0, 1).astype(BF)
    for target in range(regions):
        wanted = table_all[target, pl.ds(reg, 1), :]
        stage2[target] = jnp.dot(sent, one_hot(wanted, nodes), preferred_element_type=F32).astype(BF)
    row_copies = to_peers(
        "region", reg, regions, lambda p: stage2.at[p], lambda m: tab2.at[m], m_ssem, m_rsem
    )
    for copy in row_copies:
        copy.start()
    tab2[reg] = stage2[reg]
    set_receivers(1, whole)

    @pl.loop(0, mesh_steps)
    def begin_mesh(step):
        start_edges(step, mr_ref, mf_ref)

    for owner in range(feats):
        out_enc[owner * rows : (owner + 1) * rows, :] = enc[owner, :, pl.ds(pl.multiple_of(ft * width, width), width)]
    for copy in row_copies:
        copy.wait()
    for part in range(regions):
        fold2[
            (part // 2) * width : (part // 2 + 1) * width, (part % 2) * mcap : (part % 2 + 1) * mcap
        ] = tab2[part]

    @pl.loop(0, mesh_steps)
    def finish_mesh(step):
        finish_edges(step, ms_ref, mr_ref, fold2[...], shift_second)

    sums = share_sums(1)
    for copy in first_hops[1][1] + forwards[1] + sums:
        copy.wait()
    for layer in range(2):
        for copy in first_hops[layer][0]:
            copy.wait_send()
    result = node_rows(1, enc[ft])
    for owner in range(feats):
        proc_stage[owner] = result[:, owner * width : (owner + 1) * width]
    proc_copies = to_peers(
        "feat", ft, feats, lambda p: proc_stage.at[p], lambda m: proc_all.at[m], p_ssem, p_rsem
    )
    for copy in proc_copies:
        copy.start()
    proc_all[ft] = proc_stage[ft]
    for copy in proc_copies:
        copy.wait()
    out_proc[...] = proc_all[...].reshape(nodes, width)


def fused_device(regions, feats, *args):
    (grid_latent, mesh_latent, send_tiles, gs, gr, gf, mt, ms, mr, mf, w_send) = args[:11]
    nodes, latent = mesh_latent.shape
    width = w_send.shape[2]
    slots = send_tiles.shape[2] * TILE
    mcap = mt.shape[2]
    rows = nodes // feats
    args = list(args)
    for at in (3, 4, 7, 8):
        args[at] = args[at].reshape(1, -1)
    size = EDGE_BLOCK
    steps = max(args[3].shape[1], args[7].shape[1]) // size
    staged = [args[at] for at in (0, 10, 1, 11, 12, 13, 3, 4, 5, 6, 7, 8, 9, 15, 18, 20, 21, 22)]
    specs = [pl.BlockSpec(memory_space=pltpu.HBM)] * len(args)
    specs[2] = pl.BlockSpec(memory_space=pltpu.SMEM)
    dma = pltpu.SemaphoreType.DMA
    vm = pltpu.VMEM
    return pl.pallas_call(
        functools.partial(fused, regions, feats),
        out_shape=(jax.ShapeDtypeStruct((nodes, width), BF),) * 2,
        in_specs=specs,
        out_specs=(pl.BlockSpec(memory_space=pltpu.VMEM),) * 2,
        scratch_shapes=[
            vm((grid_latent.shape[0] // TILE, width, TILE), BF),
            vm((regions, width, slots), BF),
            vm((regions, width, slots), BF),
            vm((regions, regions, mcap), jnp.int32),
            vm((2 * width, nodes // 2), BF),
            vm((2 * width + 16, nodes // 2), F32),
            vm((width, width), F32),
            vm((2, feats, width, latent), BF),
            vm((2, feats, width, latent), BF),
            vm((2, feats, latent, width), BF),
            vm((2, feats, latent, width), BF),
            vm((feats, 2, width), F32),
            vm((2, feats, width, rows), BF),
            vm((2, feats, width, rows), BF),
            vm((feats, 1, rows), F32),
            vm((feats, rows, latent), BF),
            vm((regions, width, mcap), BF),
            vm((regions, width, mcap), BF),
            vm((regions // 2 * width, 2 * mcap), BF),
            vm((feats, rows, width), BF),
            vm((feats, rows, width), BF),
            vm((steps, slots, size), BF),
            vm((steps, nodes // 2, size), BF),
            vm((steps, width, size), F32),
            *[vm(value.shape, value.dtype) for value in staged],
            dma((len(staged),)), dma((2, 4)),
            dma((regions - 1,)), dma((regions - 1,)),
            dma((regions - 1,)), dma((regions - 1,)),
            dma((2, 3, 4)), dma((2, 3, 4)),
            dma((feats - 1,)), dma((feats - 1,)),
            dma((2, feats - 1)), dma((2, feats - 1)),
            dma((feats - 1,)), dma((feats - 1,)),
            dma((regions - 1,)), dma((regions - 1,)),
            dma((feats - 1,)), dma((feats - 1,)),
        ],
        compiler_params=pltpu.CompilerParams(
            collective_id=0, has_side_effects=True, vmem_limit_bytes=60 << 20
        ),
    )(*args)


def pick_form(regions, feats, *args):
    width = args[10].shape[2]
    even = args[3].shape[0] % EDGE_BLOCK == 0 and args[7].shape[0] % EDGE_BLOCK == 0
    rows = args[1].shape[0] // feats
    if feats == 4 and width == 128 and rows == 128 and even and regions in (2, 4):
        return fused_device(regions, feats, *args)
    return per_device(*args)


def solution(mesh):
    return jax.shard_map(
        functools.partial(pick_form, mesh.shape["region"], mesh.shape["feat"]),
        mesh=mesh,
        in_specs=(
            P(("parts", "region"), None),
            P(("parts", "region"), None),
            P(("parts", "region"), None, None),
            P(("parts", "region")),
            P(("parts", "region")),
            P(None, ("parts", "region")),
            P(("parts", "region"), None, None),
            P(("parts", "region")),
            P(("parts", "region")),
            P(None, ("parts", "region")),
            P(None, None, "feat"),
            P(None, None, "feat"),
            P(None, None, "feat"),
            P(None, "feat"),
            P(None, "feat", None),
            P(),
            P(None, None, "feat"),
            P(None, None, "feat"),
            P(None, "feat"),
            P(None, "feat", None),
            P(),
            P(),
            P(),
        ),
        out_specs=(P(("parts", "region"), "feat"), P(("parts", "region"), "feat")),
        check_vma=False,
    )
```

```python
import functools

import jax
import jax.numpy as jnp
from jax import lax
from jax.experimental import pallas as pl
from jax.experimental.pallas import tpu as pltpu
from jax.sharding import PartitionSpec as P

TILE = 128


def swish_unit(value):
    return value * jax.nn.sigmoid(value)


def layer_norm(value, gain, shift):
    center = value - jnp.mean(value, axis=-1, keepdims=True)
    spread = jnp.mean(center * center, axis=-1, keepdims=True)
    return center * lax.rsqrt(spread + 1e-05) * gain + shift


def select_rows(indices, table):
    picks = (indices[:, None] == jnp.arange(table.shape[0], dtype=jnp.int32)[None, :]).astype(
        jnp.bfloat16
    )
    return jnp.dot(picks, table, preferred_element_type=jnp.float32).astype(jnp.bfloat16)


def edge_sums(lookup, senders, receivers, features, recv_proj, w_feat, bias):
    node_count = recv_proj.shape[0]
    edge_count = senders.shape[0]
    edge_block = min(2048, edge_count)
    hidden_width = lookup.shape[1]
    node_ids = jnp.arange(node_count, dtype=jnp.int32)[:, None]
    recv_high = recv_proj.astype(jnp.bfloat16)
    recv_low = (recv_proj - recv_high.astype(jnp.float32)).astype(jnp.bfloat16)
    recv_pair = jnp.concatenate([recv_high, recv_low], axis=1)

    def visit_block(state_pair, start):
        totals, counts = state_pair
        send_part = lax.dynamic_slice_in_dim(senders, start, edge_block)
        recv_part = lax.dynamic_slice_in_dim(receivers, start, edge_block)
        feat_part = lax.dynamic_slice_in_dim(features, start, edge_block, 1)
        member = (node_ids == recv_part[None, :]).astype(jnp.bfloat16)
        picked = lax.dot_general(
            member, recv_pair, (((0,), (0,)), ((), ())), preferred_element_type=jnp.float32
        )
        recv_rows = picked[:, :hidden_width] + picked[:, hidden_width:]
        summed = lookup[send_part].astype(jnp.float32) + recv_rows
        summed = (
            summed
            + jnp.einsum("ke,kh->eh", feat_part, w_feat, precision=lax.Precision.HIGHEST)
            + bias
        )
        hidden = swish_unit(summed).astype(jnp.bfloat16)
        totals = totals + jnp.dot(member, hidden, preferred_element_type=jnp.float32)
        counts = counts + jnp.sum(member.astype(jnp.float32), axis=1)
        return ((totals, counts), None)

    starts = jnp.arange(edge_count // edge_block, dtype=jnp.int32) * edge_block
    initial = (
        jnp.zeros((node_count, hidden_width), jnp.float32),
        jnp.zeros((node_count,), jnp.float32),
    )
    result, unused = lax.scan(visit_block, initial, starts)
    return result


def node_step(
    latent,
    totals,
    counts,
    layer,
    full_outs,
    w_edge_out,
    b_edge_out,
    w_self,
    w_agg,
    b_node,
    w_node_out,
    b_node_out,
    norm_gain,
    norm_shift,
):
    summed = totals.astype(jnp.bfloat16)
    partial_agg = jnp.dot(summed, w_edge_out[layer], preferred_element_type=jnp.float32)
    gathered = (
        lax.psum(partial_agg.astype(jnp.bfloat16), "feat").astype(jnp.float32)
        + counts[:, None] * b_edge_out[layer]
    )
    preact = jnp.dot(latent, w_self[layer], preferred_element_type=jnp.float32)
    preact = (
        preact
        + jnp.dot(gathered.astype(jnp.bfloat16), w_agg[layer], preferred_element_type=jnp.float32)
        + b_node[layer]
    )
    hidden = swish_unit(preact).astype(jnp.bfloat16)
    partial_update = jnp.dot(hidden, w_node_out[layer], preferred_element_type=jnp.float32)
    update = (
        lax.psum(partial_update.astype(jnp.bfloat16), "feat").astype(jnp.float32)
        + b_node_out[layer]
    )
    return (
        latent.astype(jnp.float32) + layer_norm(update, norm_gain[layer], norm_shift[layer])
    ).astype(jnp.bfloat16)


def per_device(
    grid_latent,
    mesh_latent,
    send_tiles,
    g2m_sender,
    g2m_receiver,
    g2m_feature,
    m2m_table,
    m2m_sender,
    m2m_receiver,
    m2m_feature,
    w_send,
    w_recv,
    w_edge_feat,
    b_edge,
    w_edge_out,
    b_edge_out,
    w_self,
    w_agg,
    b_node,
    w_node_out,
    b_node_out,
    norm_gain,
    norm_shift,
):
    full_outs = (w_edge_out, w_node_out)
    node_weights = (
        full_outs,
        w_edge_out,
        b_edge_out,
        w_self,
        w_agg,
        b_node,
        w_node_out,
        b_node_out,
        norm_gain,
        norm_shift,
    )
    regions = lax.axis_size("region")
    hidden_width = w_send.shape[2]
    grid_proj = jnp.dot(grid_latent, w_send[0], preferred_element_type=jnp.float32).astype(
        jnp.bfloat16
    )
    wanted = send_tiles[0]
    tile_table = grid_proj.reshape(-1, TILE * hidden_width)
    tiles = select_rows(wanted.reshape(-1), tile_table).reshape(regions, -1, TILE * hidden_width)
    arrived = lax.all_to_all(tiles, "region", split_axis=0, concat_axis=0, tiled=True)
    grid_lookup = arrived.reshape(-1, hidden_width)
    recv_first = jnp.dot(mesh_latent, w_recv[0], preferred_element_type=jnp.float32)
    totals, counts = edge_sums(
        grid_lookup, g2m_sender, g2m_receiver, g2m_feature, recv_first, w_edge_feat[0], b_edge[0]
    )
    encoded = node_step(mesh_latent, totals, counts, 0, *node_weights)
    mesh_send = jnp.dot(encoded, w_send[1], preferred_element_type=jnp.float32).astype(jnp.bfloat16)
    everything = lax.all_gather(mesh_send, "region", axis=0, tiled=True)
    wanted = m2m_table[0]
    capacity = wanted.shape[1]
    source = m2m_sender // capacity
    row_index = wanted[source, m2m_sender % capacity]
    mesh_index = source * mesh_latent.shape[0] + jnp.maximum(row_index, 0)
    recv_second = jnp.dot(encoded, w_recv[1], preferred_element_type=jnp.float32)
    totals, counts = edge_sums(
        everything, mesh_index, m2m_receiver, m2m_feature, recv_second, w_edge_feat[1], b_edge[1]
    )
    processed = node_step(encoded, totals, counts, 1, *node_weights)
    columns = mesh_latent.shape[1] // lax.axis_size("feat")
    first_column = lax.axis_index("feat") * columns
    return (
        lax.dynamic_slice_in_dim(encoded, first_column, columns, 1),
        lax.dynamic_slice_in_dim(processed, first_column, columns, 1),
    )


MESH = pl.DeviceIdType.MESH
BF = jnp.bfloat16
EDGE_BLOCK = 4096
F32 = jnp.float32


def dot_dims(left, right, left_dim, right_dim):
    return lax.dot_general(
        left, right, (((left_dim,), (right_dim,)), ((), ())), preferred_element_type=F32
    )


def one_hot(row, count):
    ids = lax.broadcasted_iota(jnp.int32, (count, row.shape[1]), 0)
    return jnp.where(ids == row, 1.0, 0.0).astype(BF)


def swish_tanh(value):
    half = 0.5 * value
    return half + half * jnp.tanh(half)


def fused(
    regions, feats,
    grid_hbm, mesh_hbm, tiles_ref, gs_hbm, gr_hbm, gf_hbm, mt_hbm, ms_hbm, mr_hbm, mf_hbm,
    w_send_hbm, w_recv_hbm, w_ef_hbm, b_edge_hbm, weo_ref, beo_hbm, wself_ref, wagg_ref, bnode_hbm,
    wno_ref, bno_hbm, gain_hbm, shift_hbm,
    out_enc, out_proc,
    proj, stage, tab, table_all, recv_tab, acc, cols,
    weo, wno, wself, wagg, bnode, sum_stage, sum_all, cnt_stage, enc, stage2, tab2, fold2,
    proc_stage, proc_all, send_picks, recv_picks, partial_sum,
    grid_ref, w_send, mesh_ref, w_recv, w_ef, b_edge, gs_ref, gr_ref, gf_ref, mt_ref, ms_ref,
    mr_ref, mf_ref, beo, bnode_ref, bno, gain, shift, in_sem, own_sem,
    tile_send, tile_recv, id_send, id_recv, w_ssem, w_rsem, b_ssem, b_rsem, s_ssem, s_rsem,
    e_ssem, e_rsem, m_ssem, m_rsem, p_ssem, p_rsem,
):
    reg = lax.axis_index("region")
    ft = lax.axis_index("feat")
    width = w_send.shape[2]
    nodes = mesh_ref.shape[0]
    slots = tab.shape[2]
    rows = nodes // feats
    core = ft % 2
    across = (ft + 2) % feats
    partner = ft - core + (1 - core)

    loads = [
        pltpu.make_async_copy(source, target, in_sem.at[at])
        for at, (source, target) in enumerate(
            (
                (w_send_hbm, w_send), (grid_hbm, grid_ref), (mesh_hbm, mesh_ref),
                (w_recv_hbm, w_recv), (w_ef_hbm, w_ef), (b_edge_hbm, b_edge), (gs_hbm, gs_ref),
                (gr_hbm, gr_ref), (gf_hbm, gf_ref), (mt_hbm, mt_ref), (bnode_hbm, bnode_ref),
                (ms_hbm, ms_ref), (mr_hbm, mr_ref), (mf_hbm, mf_ref), (beo_hbm, beo),
                (bno_hbm, bno), (gain_hbm, gain), (shift_hbm, shift),
            )
        )
    ]
    for load in loads:
        load.start()
    barrier = pltpu.get_barrier_semaphore()
    for off in range(1, regions):
        pl.semaphore_signal(
            barrier, inc=1, device_id={"region": (reg + off) % regions}, device_id_type=MESH
        )
    for off in range(1, feats):
        pl.semaphore_signal(
            barrier, inc=1, device_id={"feat": (ft + off) % feats}, device_id_type=MESH
        )
    pl.semaphore_wait(barrier, regions + feats - 2)

    def remote(source, target, send, recv, axis, index):
        return pltpu.make_async_remote_copy(
            src_ref=source, dst_ref=target, send_sem=send, recv_sem=recv,
            device_id={axis: index}, device_id_type=MESH,
        )

    def to_peers(axis, me, count, source_of, target_of, send, recv):
        copies = []
        for off in range(1, count):
            peer = (me + off) % count
            copies.append(
                remote(source_of(peer), target_of(me), send.at[off - 1], recv.at[off - 1], axis, peer)
            )
        return copies

    id_copies = to_peers(
        "region", reg, regions, lambda p: mt_ref.at[0], lambda m: table_all.at[m], id_send, id_recv
    )
    bias_copies = to_peers(
        "feat", ft, feats, lambda p: bnode_ref, lambda m: bnode.at[m], b_ssem, b_rsem
    )
    kinds = ((weo_ref, weo), (wself_ref, wself), (wagg_ref, wagg), (wno_ref, wno))

    def weight_copies(layer, route):
        copies = []
        for kind, (own, full) in enumerate(kinds):
            slot = across if route == 2 else ft
            source = full.at[layer, slot] if route == 2 else own.at[layer]
            copies.append(
                remote(
                    source, full.at[layer, slot],
                    w_ssem.at[layer, route, kind], w_rsem.at[layer, route, kind],
                    "feat", across if route == 0 else partner,
                )
            )
        return copies

    first_hops = [[weight_copies(layer, route) for route in range(2)] for layer in range(2)]
    forwards = [weight_copies(layer, 2) for layer in range(2)]
    for route in range(2):
        for copy in first_hops[0][route]:
            copy.start()
    for load in loads[:2]:
        load.wait()

    @pl.loop(0, grid_ref.shape[0] // 512)
    def project(step):
        rows_here = grid_ref[pl.ds(step * 512, 512), :]
        block = jnp.dot(rows_here, w_send[0], preferred_element_type=F32).T.astype(BF)
        for part in range(512 // TILE):
            proj[step * (512 // TILE) + part] = block[:, part * TILE : (part + 1) * TILE]

    cap = slots // TILE
    for target in range(regions):
        for slot in range(cap):
            tile = jnp.maximum(tiles_ref[0, target, slot], 0)
            stage[target, :, slot * TILE : (slot + 1) * TILE] = proj[tile]
    tile_copies = to_peers(
        "region", reg, regions, lambda p: stage.at[p], lambda m: tab.at[m], tile_send, tile_recv
    )
    for copy in tile_copies:
        copy.start()
    for load in loads[2:]:
        load.wait()
    for copy in id_copies + bias_copies:
        copy.start()
    for route in range(2):
        for copy in first_hops[1][route]:
            copy.start()
    keeps = [
        pltpu.make_async_copy(own.at[layer], full.at[layer, ft], own_sem.at[layer, kind])
        for layer in range(2)
        for kind, (own, full) in enumerate(kinds)
    ]
    for copy in keeps:
        copy.start()
    tab[reg] = stage[reg]
    table_all[reg] = mt_ref[0]
    bnode[ft] = bnode_ref[...]

    half_nodes = nodes // 2

    def set_receivers(layer, latent):
        base = jnp.concatenate(
            [w_ef[layer], b_edge[layer : layer + 1], jnp.zeros((3, width), F32)], axis=0
        )
        turned = jnp.concatenate([base] * (width // 8), axis=0).T
        cols[...] = turned
        table = dot_dims(w_recv[layer], latent, 0, 1) + turned[:, 4:5]
        table = table.astype(BF)
        recv_tab[0:width] = table[:, :half_nodes]
        recv_tab[width:] = table[:, half_nodes:]
        acc[...] = jnp.zeros_like(acc)

    def pick_edges(step, s_ref, r_ref, shift_by):
        here = pl.ds(pl.multiple_of(step * size, size), size)
        recv = r_ref[:, here]
        low = jnp.where(recv >= half_nodes, recv - half_nodes, recv)
        recv_picks[step] = one_hot(low, half_nodes)
        local = s_ref[:, here] & ((1 << shift_by) - 1)
        send_picks[step, 0 : 1 << shift_by] = one_hot(local, 1 << shift_by)

    def start_edges(step, r_ref, f_ref):
        here = pl.ds(pl.multiple_of(step * size, size), size)
        found = jnp.dot(recv_tab[...], recv_picks[step], preferred_element_type=F32)
        value = jnp.where(r_ref[:, here] >= half_nodes, found[width:], found[:width])
        for k in range(4):
            value = value + cols[:, k : k + 1] * f_ref[k : k + 1, here]
        partial_sum[step] = value

    def finish_edges(step, s_ref, r_ref, table, shift_by):
        here = pl.ds(pl.multiple_of(step * size, size), size)
        source = s_ref[:, here] >> shift_by
        upper = r_ref[:, here] >= half_nodes
        found = jnp.dot(
            table, send_picks[step, 0 : 1 << shift_by], preferred_element_type=F32
        )
        chosen = found[:width]
        for part in range(1, table.shape[0] // width):
            chosen = jnp.where(source == part, found[part * width : (part + 1) * width], chosen)
        hidden = swish_tanh(partial_sum[step] + chosen).astype(BF)
        ids = lax.broadcasted_iota(jnp.int32, (16, size), 0)
        side = jnp.where(upper, 1, 0)
        spread = jnp.concatenate(
            [
                hidden * jnp.where(upper, 0.0, 1.0).astype(BF),
                hidden * jnp.where(upper, 1.0, 0.0).astype(BF),
                jnp.where(ids == side, 1.0, 0.0).astype(BF),
            ],
            axis=0,
        )
        acc[...] += dot_dims(spread, recv_picks[step], 1, 1)

    def share_sums(layer):
        for owner in range(feats):
            side = (owner * rows) // half_nodes
            lane = (owner * rows) % half_nodes
            sum_stage[layer, owner] = acc[
                side * width : (side + 1) * width, lane : lane + rows
            ].astype(BF)
            cnt_stage[owner] = acc[2 * width + side : 2 * width + side + 1, lane : lane + rows]
        copies = to_peers(
            "feat", ft, feats, lambda p: sum_stage.at[layer, p], lambda m: sum_all.at[layer, m],
            s_ssem.at[layer], s_rsem.at[layer],
        )
        for copy in copies:
            copy.start()
        sum_all[layer, ft] = sum_stage[layer, ft]
        return copies

    def node_rows(layer, latent):
        sums = sum_all[layer].reshape(feats * width, rows)
        agg = dot_dims(sums, weo[layer].reshape(feats * width, -1), 0, 0)
        count = jnp.broadcast_to(cnt_stage[ft], (rows, rows)).T
        agg = agg + jnp.concatenate([count] * (agg.shape[1] // rows), axis=1) * beo[layer : layer + 1]
        agg = agg.astype(BF)
        update = bno[layer : layer + 1]
        for part in range(feats):
            pre = jnp.dot(latent, wself[layer, part], preferred_element_type=F32)
            pre = pre + jnp.dot(agg, wagg[layer, part], preferred_element_type=F32)
            hidden = swish_tanh(pre + bnode[part, layer : layer + 1]).astype(BF)
            update = update + jnp.dot(hidden, wno[layer, part], preferred_element_type=F32)
        normed = layer_norm(update, gain[layer : layer + 1], shift[layer : layer + 1])
        return (latent.astype(F32) + normed).astype(BF)

    set_receivers(0, mesh_ref[...])
    size = send_picks.shape[2]
    steps = gs_ref.shape[1] // size
    shift_first = slots.bit_length() - 1

    @pl.loop(0, steps)
    def begin(step):
        pick_edges(step, gs_ref, gr_ref, shift_first)
        start_edges(step, gr_ref, gf_ref)

    for copy in tile_copies:
        copy.wait()
    for copy in first_hops[0][0]:
        copy.wait_recv()
    for copy in forwards[0]:
        copy.start()

    @pl.loop(0, steps)
    def finish(step):
        table = tab[...].reshape(regions * width, slots)
        finish_edges(step, gs_ref, gr_ref, table, shift_first)

    sums = share_sums(0)
    for copy in keeps + first_hops[0][1] + forwards[0] + sums + bias_copies:
        copy.wait()
    for copy in first_hops[1][0]:
        copy.wait_recv()
    for copy in forwards[1]:
        copy.start()
    mine = pl.ds(pl.multiple_of(ft * rows, rows), rows)
    enc[ft] = node_rows(0, mesh_ref[mine, :])
    enc_copies = [
        remote(enc.at[slot], enc.at[slot], e_ssem.at[at], e_rsem.at[at], "feat", peer)
        for at, (slot, peer) in enumerate(((ft, across), (ft, partner), (across, partner)))
    ]
    for copy in enc_copies[:2]:
        copy.start()
    mcap = tab2.shape[2]
    shift_second = (2 * mcap).bit_length() - 1
    mesh_steps = ms_ref.shape[1] // size

    @pl.loop(0, mesh_steps)
    def pick_mesh(step):
        pick_edges(step, ms_ref, mr_ref, shift_second)

    enc_copies[0].wait_recv()
    enc_copies[2].start()
    enc_copies[0].wait_send()
    for copy in id_copies + enc_copies[1:]:
        copy.wait()
    whole = enc[...].reshape(nodes, -1)
    sent = dot_dims(w_send[1], whole, 0, 1).astype(BF)
    for target in range(regions):
        wanted = table_all[target, pl.ds(reg, 1), :]
        stage2[target] = jnp.dot(sent, one_hot(wanted, nodes), preferred_element_type=F32).astype(BF)
    row_copies = to_peers(
        "region", reg, regions, lambda p: stage2.at[p], lambda m: tab2.at[m], m_ssem, m_rsem
    )
    for copy in row_copies:
        copy.start()
    tab2[reg] = stage2[reg]
    set_receivers(1, whole)

    @pl.loop(0, mesh_steps)
    def begin_mesh(step):
        start_edges(step, mr_ref, mf_ref)

    for owner in range(feats):
        out_enc[owner * rows : (owner + 1) * rows, :] = enc[owner, :, pl.ds(pl.multiple_of(ft * width, width), width)]
    for copy in row_copies:
        copy.wait()
    for part in range(regions):
        fold2[
            (part // 2) * width : (part // 2 + 1) * width, (part % 2) * mcap : (part % 2 + 1) * mcap
        ] = tab2[part]

    @pl.loop(0, mesh_steps)
    def finish_mesh(step):
        finish_edges(step, ms_ref, mr_ref, fold2[...], shift_second)

    sums = share_sums(1)
    for copy in first_hops[1][1] + forwards[1] + sums:
        copy.wait()
    for layer in range(2):
        for copy in first_hops[layer][0]:
            copy.wait_send()
    result = node_rows(1, enc[ft])
    for owner in range(feats):
        proc_stage[owner] = result[:, owner * width : (owner + 1) * width]
    proc_copies = to_peers(
        "feat", ft, feats, lambda p: proc_stage.at[p], lambda m: proc_all.at[m], p_ssem, p_rsem
    )
    for copy in proc_copies:
        copy.start()
    proc_all[ft] = proc_stage[ft]
    for copy in proc_copies:
        copy.wait()
    out_proc[...] = proc_all[...].reshape(nodes, width)


def fused_device(regions, feats, *args):
    (grid_latent, mesh_latent, send_tiles, gs, gr, gf, mt, ms, mr, mf, w_send) = args[:11]
    nodes, latent = mesh_latent.shape
    width = w_send.shape[2]
    slots = send_tiles.shape[2] * TILE
    mcap = mt.shape[2]
    rows = nodes // feats
    args = list(args)
    for at in (3, 4, 7, 8):
        args[at] = args[at].reshape(1, -1)
    size = EDGE_BLOCK
    steps = max(args[3].shape[1], args[7].shape[1]) // size
    staged = [args[at] for at in (0, 10, 1, 11, 12, 13, 3, 4, 5, 6, 7, 8, 9, 15, 18, 20, 21, 22)]
    specs = [pl.BlockSpec(memory_space=pltpu.HBM)] * len(args)
    specs[2] = pl.BlockSpec(memory_space=pltpu.SMEM)
    dma = pltpu.SemaphoreType.DMA
    vm = pltpu.VMEM
    return pl.pallas_call(
        functools.partial(fused, regions, feats),
        out_shape=(jax.ShapeDtypeStruct((nodes, width), BF),) * 2,
        in_specs=specs,
        out_specs=(pl.BlockSpec(memory_space=pltpu.VMEM),) * 2,
        scratch_shapes=[
            vm((grid_latent.shape[0] // TILE, width, TILE), BF),
            vm((regions, width, slots), BF),
            vm((regions, width, slots), BF),
            vm((regions, regions, mcap), jnp.int32),
            vm((2 * width, nodes // 2), BF),
            vm((2 * width + 16, nodes // 2), F32),
            vm((width, width), F32),
            vm((2, feats, width, latent), BF),
            vm((2, feats, width, latent), BF),
            vm((2, feats, latent, width), BF),
            vm((2, feats, latent, width), BF),
            vm((feats, 2, width), F32),
            vm((2, feats, width, rows), BF),
            vm((2, feats, width, rows), BF),
            vm((feats, 1, rows), F32),
            vm((feats, rows, latent), BF),
            vm((regions, width, mcap), BF),
            vm((regions, width, mcap), BF),
            vm((regions // 2 * width, 2 * mcap), BF),
            vm((feats, rows, width), BF),
            vm((feats, rows, width), BF),
            vm((steps, slots, size), BF),
            vm((steps, nodes // 2, size), BF),
            vm((steps, width, size), F32),
            *[vm(value.shape, value.dtype) for value in staged],
            dma((len(staged),)), dma((2, 4)),
            dma((regions - 1,)), dma((regions - 1,)),
            dma((regions - 1,)), dma((regions - 1,)),
            dma((2, 3, 4)), dma((2, 3, 4)),
            dma((feats - 1,)), dma((feats - 1,)),
            dma((2, feats - 1)), dma((2, feats - 1)),
            dma((feats - 1,)), dma((feats - 1,)),
            dma((regions - 1,)), dma((regions - 1,)),
            dma((feats - 1,)), dma((feats - 1,)),
        ],
        compiler_params=pltpu.CompilerParams(
            collective_id=0, has_side_effects=True, vmem_limit_bytes=60 << 20
        ),
    )(*args)


def pick_form(regions, feats, *args):
    width = args[10].shape[2]
    even = args[3].shape[0] % EDGE_BLOCK == 0 and args[7].shape[0] % EDGE_BLOCK == 0
    rows = args[1].shape[0] // feats
    if feats == 4 and width == 128 and rows == 128 and even and regions in (2, 4):
        return fused_device(regions, feats, *args)
    return per_device(*args)


def solution(mesh):
    return jax.shard_map(
        functools.partial(pick_form, mesh.shape["region"], mesh.shape["feat"]),
        mesh=mesh,
        in_specs=(
            P(("parts", "region"), None),
            P(("parts", "region"), None),
            P(("parts", "region"), None, None),
            P(("parts", "region")),
            P(("parts", "region")),
            P(None, ("parts", "region")),
            P(("parts", "region"), None, None),
            P(("parts", "region")),
            P(("parts", "region")),
            P(None, ("parts", "region")),
            P(None, None, "feat"),
            P(None, None, "feat"),
            P(None, None, "feat"),
            P(None, "feat"),
            P(None, "feat", None),
            P(),
            P(None, None, "feat"),
            P(None, None, "feat"),
            P(None, "feat"),
            P(None, "feat", None),
            P(),
            P(),
            P(),
        ),
        out_specs=(P(("parts", "region"), "feat"), P(("parts", "region"), "feat")),
        check_vma=False,
    )
```
